256 devices in a mesh: expert: 64 (over x, y_hi, z), tensor: 4 (over y_lo, core).
Axes of the slice: x: 4, y: 4 (y_hi: 2, y_lo: 2; y = y_hi * 2 + y_lo), z: 8, core: 2. Of those that a mesh axis runs over, the one named last changes fastest.
Arguments:
- tokens: bfloat16 [8192, 4096], P('expert', 'tensor'), may hold values from -6 to 6
- expert_ids: int32 [8192, 8], P('expert'), may hold values from 0 to 63, as said below
- slot_index: int32 [8192, 8], P('expert'), may hold values from -1 to 15, as said below
- gate_fixed: int32 [8192, 8], P('expert'), may hold values from 1024 to 32767
- gate_weight: bfloat16 [64, 4096, 1536], P('expert', None, 'tensor'), may hold values from -0.09375 to 0.09375
- up_weight: bfloat16 [64, 4096, 1536], P('expert', None, 'tensor'), may hold values from -0.09375 to 0.09375
- down_weight: bfloat16 [64, 1536, 4096], P('expert', 'tensor'), may hold values from -0.15625 to 0.15625
Outputs:
- moe_out: bfloat16 [8192, 4096], P('expert', 'tensor')
The draws below stay inside these ranges and needn't reach their ends.
Inputs may be any that keep to these rules, and one draw needn't show every extreme that they name: `expert_ids`: each token names 8 different experts. One expert, drawn anew in every draw, is named by every token. `slot_index`: within each group of 128 consecutive tokens and each expert, the choices that name the expert, taken in a priority order of the group's tokens drawn anew in every draw, get slots 0, 1, 2 and so on; those past slot 15 get -1. No two choices of one group and expert share a slot. In every draw some expert fills all 16 slots in every group.
All inputs are finite; a program needn't handle non-finite values.
Results may differ from the reference program's by a relative error of at most 0.017.
Values may be sent and summed in bfloat16 or wider, within the bound.
A program may use at most 128 MiB of HBM per device.

```python
import jax
import jax.numpy as jnp
from jax import lax

D = 4096
FF = 1536
TOP = 8
TOK_DEV = 128
EXPERTS = 64
CAP = 16
TOKENS = 8192
FF_PART = 384


def routing(key):
    base = jax.random.fold_in(key, 101)
    key_hot, key_bias, key_noise, key_order, key_perm = jax.random.split(base, 5)
    hot_expert = jax.random.randint(key_hot, (), 0, EXPERTS)
    expert_range = jnp.arange(EXPERTS, dtype=jnp.int32)
    bias = jax.random.randint(key_bias, (EXPERTS,), 0, 2 ** 14)
    bias = jnp.where(expert_range == hot_expert, 2 ** 20, bias)
    noise = jax.random.randint(key_noise, (TOKENS, EXPERTS), 0, 2 ** 16)
    score = (noise + bias[None, :]) * EXPERTS + expert_range[None, :]
    unused, chosen = lax.top_k(score, TOP)
    order_score = jax.random.randint(key_order, (TOKENS, TOP), 0, 2 ** 16) * TOP + jnp.arange(TOP, dtype=jnp.int32)[None, :]
    unused_two, order = lax.top_k(order_score, TOP)
    chosen = jnp.take_along_axis(chosen, order, axis=1).astype(jnp.int32)
    groups = TOKENS // TOK_DEV
    perm_keys = jax.random.split(key_perm, groups)
    token_order = jax.vmap(lambda k: jax.random.permutation(k, TOK_DEV))(perm_keys).astype(jnp.int32)
    inverse = jnp.argsort(token_order, axis=1, stable=True).astype(jnp.int32)
    grouped = chosen.reshape(groups, TOK_DEV, TOP)
    reordered = jnp.take_along_axis(grouped, token_order[:, :, None], axis=1)
    blocks = reordered.reshape(groups, TOK_DEV * TOP)
    onehot = (blocks[:, :, None] == expert_range[None, None, :]).astype(jnp.int32)
    running = jnp.cumsum(onehot, axis=1)
    rank_of = jnp.sum(running * onehot, axis=2) - 1
    slots = jnp.where(rank_of < CAP, rank_of, -1).astype(jnp.int32)
    slots = slots.reshape(groups, TOK_DEV, TOP)
    slots = jnp.take_along_axis(slots, inverse[:, :, None], axis=1).astype(jnp.int32)
    return (chosen, slots.reshape(TOKENS, TOP))


def draw_expert_ids(key, part):
    return routing(key)[0]


def draw_slot_index(key, part):
    return routing(key)[1]


def plant(values, rng, least, high):
    spot = [jax.random.randint(jax.random.fold_in(rng, axis), (), 0, length) for axis, length in enumerate(values.shape)]
    widest = values.shape.index(max(values.shape))
    beside = spot[:widest] + [(spot[widest] + 1) % values.shape[widest]] + spot[widest + 1:]
    return values.at[tuple(spot)].set(least).at[tuple(beside)].set(high)


def level_of(stream_key, dims, pieces, least, high):
    def one(dim, shards_of):
        draws = jax.random.uniform(jax.random.fold_in(jax.random.fold_in(stream_key, 6), dim), (shards_of,), jnp.float32, least / len(pieces), high / len(pieces))
        return jnp.repeat(jnp.exp(draws), dims[dim] // shards_of).reshape((-1,) + (1,) * (len(dims) - dim - 1))

    gain = one(*pieces[0])
    for cut in pieces[1:]:
        gain = gain * one(*cut)
    return gain


def bell_draw(own_key, dims, deviation, limit, cuts=(), held_as=jnp.bfloat16):
    entries = deviation * jax.random.normal(own_key, dims, jnp.float32)
    if cuts:
        entries = entries * level_of(own_key, dims, cuts, -0.22, 0.18)
    return jnp.clip(entries, -limit, limit).astype(held_as)


def setup_inputs(seed: int = 0) -> dict:
    key_of = jax.random.split(jax.random.key(seed), 8)
    return {
        "tokens": bell_draw(key_of[0], (TOKENS, D), 1.0, 6.0, ((0, 64), (1, 4))),
        "expert_ids": draw_expert_ids(jax.random.fold_in(key_of[7], 71), 0),
        "slot_index": draw_slot_index(jax.random.fold_in(key_of[7], 71), 0),
        "gate_fixed": plant(jax.random.randint(key_of[3], (TOKENS, TOP), 1024, 32768), jax.random.fold_in(key_of[3], 1), 1024, 32767).astype(jnp.int32),
        "gate_weight": bell_draw(key_of[4], (EXPERTS, D, FF), D ** -0.5, 0.09375, ((0, 64), (2, 4))),
        "up_weight": bell_draw(key_of[5], (EXPERTS, D, FF), D ** -0.5, 0.09375, ((0, 64), (2, 4))),
        "down_weight": bell_draw(key_of[6], (EXPERTS, FF, D), FF ** -0.5, 0.15625, ((0, 64), (1, 4))),
    }


def expert_block(routed, gate_w, up_w, down_w):
    gate_act = jnp.dot(routed, gate_w, preferred_element_type=jnp.float32)
    up_act = jnp.dot(routed, up_w, preferred_element_type=jnp.float32)
    hidden = (jax.nn.silu(gate_act) * up_act).astype(jnp.bfloat16)
    total = jnp.zeros((routed.shape[0], down_w.shape[1]), jnp.float32)
    for quarter in range(FF // FF_PART):
        lower = quarter * FF_PART
        partial_value = jnp.dot(hidden[:, lower:lower + FF_PART], down_w[lower:lower + FF_PART], preferred_element_type=jnp.float32)
        total = total + lax.optimization_barrier(partial_value.astype(jnp.bfloat16)).astype(jnp.float32)
    return total.astype(jnp.bfloat16)


def reference(tokens, expert_ids, slot_index, gate_fixed, gate_weight, up_weight, down_weight):
    groups = TOKENS // TOK_DEV
    pair_count = TOK_DEV * TOP
    ids_flat = expert_ids.reshape(groups, pair_count)
    slots_flat = slot_index.reshape(groups, pair_count)
    gate_vals = jnp.where(slots_flat >= 0, gate_fixed.reshape(groups, pair_count).astype(jnp.float32) / 32768.0, 0.0)
    local_token = (jnp.arange(pair_count, dtype=jnp.int32) // TOP).astype(jnp.int32)
    position = jnp.where(slots_flat >= 0, ids_flat * CAP + slots_flat, EXPERTS * CAP).astype(jnp.int32)
    offsets = (jnp.arange(groups, dtype=jnp.int32) * TOK_DEV).astype(jnp.int32)

    def one_group(place, weights_in, offset):
        owner = jnp.full((EXPERTS * CAP,), TOKENS, jnp.int32).at[place].set(local_token + offset, mode="drop")
        weight_row = jnp.zeros((EXPERTS * CAP,), jnp.float32).at[place].set(weights_in, mode="drop")
        return owner, weight_row

    owners, slot_weights = jax.vmap(one_group)(position, gate_vals, offsets)
    owners = owners.reshape(groups, EXPERTS, CAP).transpose(1, 0, 2).reshape(EXPERTS, groups * CAP)
    slot_weights = slot_weights.reshape(groups, EXPERTS, CAP).transpose(1, 0, 2).reshape(EXPERTS, groups * CAP)

    def one_expert(accum, inputs):
        gate_w, up_w, down_w, owner, weight_row = inputs
        filled = owner < TOKENS
        picked = tokens[jnp.minimum(owner, TOKENS - 1)]
        routed = jnp.where(filled[:, None], picked, jnp.zeros((), picked.dtype))
        result = expert_block(routed, gate_w, up_w, down_w)
        widened = lax.optimization_barrier(result).astype(jnp.float32)
        accum = accum.at[owner].add(weight_row[:, None] * widened, mode="drop")
        return accum, None

    start = jnp.zeros((TOKENS, D), jnp.float32)
    accum, unused = lax.scan(one_expert, start, (gate_weight, up_weight, down_weight, owners, slot_weights))
    return accum.astype(jnp.bfloat16)
```

```python
import functools

import jax
import jax.numpy as jnp
from jax import lax
from jax.experimental import pallas as pl
from jax.experimental.pallas import tpu as pltpu
from jax.sharding import PartitionSpec as P

CAP = 16
MESH = pl.DeviceIdType.MESH
BF16 = jnp.bfloat16
F32 = jnp.float32


def kernel(
    nx,
    nz,
    order,
    tok_ref,
    meta_ref,
    gate_hbm,
    up_hbm,
    down_hbm,
    out_ref,
    w1,
    wd,
    metas,
    zb,
    sel,
    xb,
    acc,
    hid,
    po,
    cr,
    ts,
    tr,
    ys,
    rb,
    zs,
    zr,
    w_sem,
    meta_send,
    meta_recv,
    zb_send,
    zb_recv,
    sel_send,
    sel_recv,
    t_send,
    t_recv,
    c1_send,
    c1_recv,
    c2_send,
    c2_recv,
    ce_send,
    ce_recv,
    tt_send,
    tt_recv,
    r_send,
    r_recv,
    zr_send,
    zr_recv,
):
    expert = lax.axis_index("expert")
    tensor = lax.axis_index("tensor")
    z = lax.rem(expert, nz)
    yh = lax.rem(expert // nz, 2)
    x = expert // (2 * nz)
    c = lax.rem(tensor, 2)
    yl = tensor // 2
    half = nz // 2
    tok, width = tok_ref.shape
    hw = width // 2
    hidden = hid.shape[1]
    own_q = tensor
    far_q = (1 - yl) * 2 + c

    def at_z(d):
        return (expert - z + lax.rem(z + d + nz, nz), tensor)

    def at_plane(xx, rel):
        if rel == 0:
            return ((xx * 2 + yh) * nz + z, tensor)
        return ((xx * 2 + 1 - yh) * nz + z, (1 - yl) * 2 + c)

    t_peer = (expert, far_q)
    c_peer = (expert, yl * 2 + 1 - c)

    def blocks(s):
        if s == 0:
            return 0, 1
        if s == half:
            return nz - 1, 1
        return 2 * s - 1, 2

    def remote(src, dst, send, recv, dev):
        return pltpu.make_async_remote_copy(
            src_ref=src,
            dst_ref=dst,
            send_sem=send,
            recv_sem=recv,
            device_id=dev,
            device_id_type=MESH,
        )

    def wait_bytes(ref, sem):
        pltpu.make_async_copy(ref, ref, sem).wait()

    loads = []
    for q in range(4):
        rows = pl.ds(q * width, width)
        loads.append(
            pltpu.make_async_copy(
                gate_hbm.at[0, rows, :], w1.at[q, :, pl.ds(0, hidden)], w_sem.at[q]
            )
        )
        loads.append(
            pltpu.make_async_copy(
                up_hbm.at[0, rows, :], w1.at[q, :, pl.ds(hidden, hidden)], w_sem.at[4 + q]
            )
        )
        loads.append(
            pltpu.make_async_copy(down_hbm.at[0, :, rows], wd.at[q], w_sem.at[8 + q])
        )
    for load in loads:
        load.start()

    barrier = pltpu.get_barrier_semaphore()
    peers = [at_z(d) for d in range(1, nz)]
    peers += [at_plane(lax.rem(x + d, nx), 0) for d in range(1, nx)]
    peers += [at_plane(lax.rem(x + d, nx), 1) for d in range(nx)]
    peers += [t_peer, c_peer]
    for peer in peers:
        pl.semaphore_signal(barrier, inc=1, device_id=peer, device_id_type=MESH)
    pl.semaphore_wait(barrier, len(peers))

    ends = []

    for d in range(1, nz):
        remote(meta_ref, metas.at[d], meta_send, meta_recv, at_z(d)).start()
    ends.append(lambda: wait_bytes(metas.at[pl.ds(1, nz - 1)], meta_send))
    metas[0] = meta_ref[...]

    def z_copies(s):
        if s == half:
            f_src = tok_ref if s == 1 else zb.at[2 * s - 3]
            b_src = tok_ref if s == 1 else zb.at[2 * s - 2]
            lo, hi = pl.ds(0, hw), pl.ds(hw, hw)
            return (
                remote(f_src.at[:, lo], zb.at[nz - 1, :, lo], zb_send.at[s, 0], zb_recv.at[s, 0], at_z(1)),
                remote(b_src.at[:, hi], zb.at[nz - 1, :, hi], zb_send.at[s, 1], zb_recv.at[s, 1], at_z(-1)),
            )
        f_src = tok_ref if s == 1 else zb.at[2 * s - 3]
        b_src = tok_ref if s == 1 else zb.at[2 * s - 2]
        return (
            remote(f_src, zb.at[2 * s - 1], zb_send.at[s, 0], zb_recv.at[s, 0], at_z(1)),
            remote(b_src, zb.at[2 * s], zb_send.at[s, 1], zb_recv.at[s, 1], at_z(-1)),
        )

    def z_send(s):
        for copy in z_copies(s):
            copy.start()
            ends.append(copy.wait_send)

    z_send(1)

    def delta(b):
        if b == 0:
            return 0
        if b == nz - 1:
            return half
        return (b + 1) // 2 if b % 2 == 1 else nz - b // 2

    seat = 2 * nx * CAP
    per_rel = nx * CAP

    def seat_codes():
        j = lax.broadcasted_iota(jnp.int32, (seat, tok), 0)
        rel = j // per_rel
        rest = j - rel * per_rel
        xe = rest // CAP
        slot = rest - xe * CAP
        far = yh + rel - 2 * yh * rel
        return ((xe * 2 + far) * nz + z) * CAP + slot

    state = {"meta": False}

    def stage_a(s):
        first, count = blocks(s)
        if s > 0:
            for copy in z_copies(s):
                copy.wait_recv()
            if s < half:
                z_send(s + 1)
            if not state["meta"]:
                wait_bytes(metas.at[pl.ds(1, nz - 1)], meta_recv)
                state["meta"] = True
        code = seat_codes()
        for b in range(first, first + count):
            pick = jnp.zeros((seat, tok), F32)
            for k in range(8):
                pick = jnp.where(metas[delta(b), pl.ds(k, 1), :] == code, 1.0, pick)
            src = tok_ref[...] if b == 0 else zb[b]
            rows = jnp.dot(pick.astype(BF16), src, preferred_element_type=F32).astype(BF16)
            sel[0, b] = rows[:per_rel]
            sel[1, b] = rows[per_rel:]
        bl = pl.ds(first, count)
        mine = pl.ds(pl.multiple_of(x * CAP, CAP), CAP)
        pltpu.make_async_copy(
            sel.at[0, bl, mine, :], xb.at[own_q, 0, bl, mine, :], sel_recv.at[s, 0]
        ).start()
        for rel in range(2):
            for d in range(1 - rel, nx):
                xx = lax.rem(x + d, nx)
                theirs = pl.ds(pl.multiple_of(xx * CAP, CAP), CAP)
                remote(
                    sel.at[rel, bl, theirs, :],
                    xb.at[own_q, rel, bl, mine, :],
                    sel_send.at[s, rel],
                    sel_recv.at[s, rel],
                    at_plane(xx, rel),
                ).start()
        ends.append(
            lambda: wait_bytes(sel.at[0, bl, pl.ds(0, per_rel - CAP), :], sel_send.at[s, 0])
        )
        ends.append(lambda: wait_bytes(sel.at[1, bl], sel_send.at[s, 1]))

    def t_copies(s):
        bl = pl.ds(*blocks(s))
        out = []
        for rel in range(2):
            ref = xb.at[own_q if rel == 0 else far_q, rel, bl]
            out.append(remote(ref, ref, t_send.at[s, rel], t_recv.at[s, rel], t_peer))
        return out

    def c_copies(s, late):
        bl = pl.ds(*blocks(s))
        send, recv = (c2_send, c2_recv) if late else (c1_send, c1_recv)
        out = []
        for rel in range(2):
            ref = xb.at[own_q if (rel == 0) != late else far_q, rel, bl]
            out.append(remote(ref, ref, send.at[s, rel], recv.at[s, rel], c_peer))
        return out

    def start_all(copies):
        for copy in copies:
            copy.start()
            ends.append(copy.wait_send)

    def stage_b(s):
        bl = pl.ds(*blocks(s))
        t_list, c_list = t_copies(s), c_copies(s, False)
        for rel in range(2):
            wait_bytes(xb.at[own_q if rel == 0 else far_q, rel, bl], sel_recv.at[s, rel])
            start_all([t_list[rel], c_list[rel]])

    def stage_c(s):
        t_list, c_list = t_copies(s), c_copies(s, True)
        for rel in range(2):
            t_list[rel].wait_recv()
            start_all([c_list[rel]])

    def ce_copies(s):
        bl = pl.ds(*blocks(s))
        return [
            remote(
                po.at[2 * p + 1 - c, :, bl],
                cr.at[p, :, bl],
                ce_send.at[s, p],
                ce_recv.at[s, p],
                c_peer,
            )
            for p in range(2)
        ]

    loaded = {"w1": False, "wd": False}

    def stage_d(s):
        first, count = blocks(s)
        bl = pl.ds(first, count)
        rows = count * seat
        for late in (False, True):
            for copy in c_copies(s, late):
                copy.wait_recv()
        if not loaded["w1"]:
            loaded["w1"] = True
            for load in loads:
                load.wait()

        def up_step(q, carry):
            part = jnp.dot(
                xb[q, :, bl].reshape(rows, width), w1[q], preferred_element_type=F32
            )
            acc[pl.ds(0, rows), :] += part
            return carry

        acc[pl.ds(0, rows), :] = jnp.zeros((rows, 2 * hidden), F32)
        lax.fori_loop(0, 4, up_step, 0)
        gate = acc[pl.ds(0, rows), pl.ds(0, hidden)]
        up = acc[pl.ds(0, rows), pl.ds(hidden, hidden)]
        hid[pl.ds(0, rows), :] = (gate / (1.0 + jnp.exp(-gate)) * up).astype(BF16)

        def down_step(p, core):
            q = 2 * p + core
            part = jnp.dot(hid[pl.ds(0, rows), :], wd[q], preferred_element_type=F32)
            po[q, :, bl] = part.astype(BF16).reshape(2, count, per_rel, width)
            return core

        lax.fori_loop(0, 2, down_step, 1 - c)
        start_all(ce_copies(s))
        lax.fori_loop(0, 2, down_step, c)

    def tt_copies(s):
        bl = pl.ds(*blocks(s))
        return [
            remote(ts.at[rel, bl], tr.at[rel, bl], tt_send.at[s, rel], tt_recv.at[s, rel], t_peer)
            for rel in range(2)
        ]

    def stage_f(s):
        bl = pl.ds(*blocks(s))
        copies = tt_copies(s)
        for copy in ce_copies(s):
            copy.wait_recv()
        for rel in range(2):
            p = 1 - yl if rel == 0 else yl
            both = po[2 * p + c, rel, bl].astype(F32) + cr[p, rel, bl].astype(F32)
            ts[rel, bl] = both.astype(BF16)
            start_all([copies[rel]])

    def stage_g(s):
        bl = pl.ds(*blocks(s))
        copies = tt_copies(s)
        mine = pl.ds(pl.multiple_of(x * CAP, CAP), CAP)
        for rel in range(2):
            p = yl if rel == 0 else 1 - yl
            copies[rel].wait_recv()
            total = po[2 * p + c, rel, bl].astype(F32) + cr[p, rel, bl].astype(F32)
            ys[rel, bl] = (total + tr[rel, bl].astype(F32)).astype(BF16)
            if rel == 0:
                pltpu.make_async_copy(
                    ys.at[0, bl, mine, :], rb.at[0, bl, mine, :], r_recv.at[s, 0]
                ).start()
            for d in range(1 - rel, nx):
                xx = lax.rem(x + d, nx)
                theirs = pl.ds(pl.multiple_of(xx * CAP, CAP), CAP)
                remote(
                    ys.at[rel, bl, theirs, :],
                    rb.at[rel, bl, mine, :],
                    r_send.at[s, rel],
                    r_recv.at[s, rel],
                    at_plane(xx, rel),
                ).start()
        ends.append(
            lambda: wait_bytes(ys.at[0, bl, pl.ds(0, per_rel - CAP), :], r_send.at[s, 0])
        )
        ends.append(lambda: wait_bytes(ys.at[1, bl], r_send.at[s, 1]))

    def back_copies(s):
        if s == half:
            b = nz - 1
            lo, hi = pl.ds(0, hw), pl.ds(hw, hw)
            return (
                remote(zs.at[b, :, lo], zr.at[b, :, lo], zr_send.at[s, 0], zr_recv.at[s, 0], at_z(-1)),
                remote(zs.at[b, :, hi], zr.at[b, :, hi], zr_send.at[s, 1], zr_recv.at[s, 1], at_z(1)),
            )
        return (
            remote(zs.at[2 * s - 1], zr.at[2 * s - 1], zr_send.at[s, 0], zr_recv.at[s, 0], at_z(-1)),
            remote(zs.at[2 * s], zr.at[2 * s], zr_send.at[s, 1], zr_recv.at[s, 1], at_z(1)),
        )

    def stage_h(s):
        first, count = blocks(s)
        bl = pl.ds(first, count)
        for rel in range(2):
            wait_bytes(rb.at[rel, bl], r_recv.at[s, rel])
        code = seat_codes()
        arrived = back_copies(s + 1) if s < half else None
        copies = back_copies(s) if s > 0 else None
        sums = []
        for b in range(first, first + count):
            high = jnp.zeros((seat, tok), F32)
            low = jnp.zeros((seat, tok), F32)
            for k in range(8):
                hit = metas[delta(b), pl.ds(k, 1), :] == code
                weight = metas[delta(b), pl.ds(8 + k, 1), :]
                top = weight // 128
                high = jnp.where(hit, top.astype(F32) / 256.0, high)
                low = jnp.where(hit, (weight - top * 128).astype(F32) / 32768.0, low)
            rows = jnp.concatenate([rb[0, b], rb[1, b]], axis=0)
            dims = (((0,), (0,)), ((), ()))
            total = lax.dot_general(high.astype(BF16), rows, dims, preferred_element_type=F32)
            total += lax.dot_general(low.astype(BF16), rows, dims, preferred_element_type=F32)
            if s == 0:
                for i in range(2):
                    arrived[i].wait_recv()
                if half == 1:
                    total += zr[nz - 1].astype(F32)
                else:
                    total += zr[1].astype(F32) + zr[2].astype(F32)
                out_ref[...] = total.astype(BF16)
                return
            if s == half:
                zs[b] = total.astype(BF16)
                start_all(copies)
                return
            i = b - first
            arrived[i].wait_recv()
            if s == half - 1:
                lo, hi = pl.ds(0, hw), pl.ds(hw, hw)
                if i == 0:
                    zs[b, :, lo] = (total[:, :hw] + zr[nz - 1, :, lo].astype(F32)).astype(BF16)
                    zs[b, :, hi] = total[:, hw:].astype(BF16)
                else:
                    zs[b, :, lo] = total[:, :hw].astype(BF16)
                    zs[b, :, hi] = (total[:, hw:] + zr[nz - 1, :, hi].astype(F32)).astype(BF16)
            else:
                zs[b] = (total + zr[2 * (s + 1) - 1 + i].astype(F32)).astype(BF16)
            start_all([copies[i]])

    stages = {
        "A": stage_a,
        "B": stage_b,
        "C": stage_c,
        "D": stage_d,
        "F": stage_f,
        "G": stage_g,
        "H": stage_h,
    }
    for name, s in order:
        stages[name](s)
    for end in ends:
        end()


def make_order(half):
    order = [("A", 0), ("B", 0), ("A", 1), ("B", 1), ("C", 0), ("D", 0)]
    for s in range(2, half + 1):
        order += [("A", s), ("B", s), ("C", s - 1)]
        order += [("D", s - 1)]
    order += [("C", half)]
    order += [("F", half - 1), ("D", half), ("F", half)]
    order += [("F", s) for s in range(half - 2, -1, -1)]
    order += [("G", half - 1), ("G", half), ("H", half), ("H", half - 1)]
    for s in range(half - 2, -1, -1):
        order += [("G", s), ("H", s)]
    return order


def moe(nx, nz, tokens, meta, gate_weight, up_weight, down_weight):
    tok, width = tokens.shape
    hidden = gate_weight.shape[2]
    half = nz // 2
    chunks = half + 1
    per_rel = nx * CAP
    rows = 4 * per_rel
    dma = pltpu.SemaphoreType.DMA
    pairs = dma((chunks, 2))
    vmem = pl.BlockSpec(memory_space=pltpu.VMEM)
    hbm = pl.BlockSpec(memory_space=pl.ANY)
    scratch = [
        pltpu.VMEM((4, width, 2 * hidden), BF16),
        pltpu.VMEM((4, hidden, width), BF16),
        pltpu.VMEM((nz, 16, tok), jnp.int32),
        pltpu.VMEM((nz, tok, width), BF16),
        pltpu.VMEM((2, nz, per_rel, width), BF16),
        pltpu.VMEM((4, 2, nz, per_rel, width), BF16),
        pltpu.VMEM((rows, 2 * hidden), F32),
        pltpu.VMEM((rows, hidden), BF16),
        pltpu.VMEM((4, 2, nz, per_rel, width), BF16),
        pltpu.VMEM((2, 2, nz, per_rel, width), BF16),
        pltpu.VMEM((2, nz, per_rel, width), BF16),
        pltpu.VMEM((2, nz, per_rel, width), BF16),
        pltpu.VMEM((2, nz, per_rel, width), BF16),
        pltpu.VMEM((2, nz, per_rel, width), BF16),
        pltpu.VMEM((nz, tok, width), BF16),
        pltpu.VMEM((nz, tok, width), BF16),
        dma((12,)),
        dma,
        dma,
    ] + [pairs] * 18
    return pl.pallas_call(
        functools.partial(kernel, nx, nz, make_order(half)),
        out_shape=jax.ShapeDtypeStruct((tok, width), BF16),
        in_specs=[vmem, vmem, hbm, hbm, hbm],
        out_specs=vmem,
        scratch_shapes=scratch,
        compiler_params=pltpu.CompilerParams(
            collective_id=0,
            has_side_effects=True,
            vmem_limit_bytes=60 * 1024 * 1024,
        ),
    )(tokens, meta, gate_weight, up_weight, down_weight)


def shards(nx, nz, tokens, expert_ids, slot_index, gate_fixed, gate_weight, up_weight, down_weight):
    place = jnp.where(slot_index >= 0, expert_ids * CAP + slot_index, -1)
    meta = jnp.concatenate([place.T, gate_fixed.T], axis=0)
    return moe(nx, nz, tokens, meta, gate_weight, up_weight, down_weight)


def solution(mesh, nx=4, nz=8):
    in_specs = (
        P("expert", "tensor"),
        P("expert", None),
        P("expert", None),
        P("expert", None),
        P("expert", None, "tensor"),
        P("expert", None, "tensor"),
        P("expert", "tensor", None),
    )
    return jax.shard_map(
        functools.partial(shards, nx, nz),
        mesh=mesh,
        in_specs=in_specs,
        out_specs=P("expert", "tensor"),
        check_vma=False,
    )
```

```python
import functools

import jax
import jax.numpy as jnp
from jax import lax
from jax.experimental import pallas as pl
from jax.experimental.pallas import tpu as pltpu
from jax.sharding import PartitionSpec as P

CAP = 16
MESH = pl.DeviceIdType.MESH
BF16 = jnp.bfloat16
F32 = jnp.float32


D_COUNT = 2
R_COUNT = 2
ORDERS = {
    4: [
        "B0ab A1a C0ab A1b",
        "B1a U0 V0 A2a",
        "B1b A2b C1a B2a",
        "C1b A3a B2b U1",
        "A3b V1 B3a C2a",
        "B3b C2b A4ab U2",
        "V2 B4a C3a B4b",
        "C3b U3 V3 C4ab",
        "F3ba U4 V4 F4ba",
        "F2ba F1ba F0ba G3ba",
        "G4ba H4ba H3ba G2ba",
        "H2ba G1b G1a H1b",
        "G0b H1a G0a H0ba",
    ],
    1: [
        "B0ab A1ab B1ab C0ab",
        "U0 V0 C1ab U1",
        "V1 F0ba F1ba G0ba",
        "G1ba H1ba H0ba",
    ],
    2: [
        "B0ab A1a C0ab A1b",
        "B1a U0 V0 A2a",
        "B1b A2b C1a B2a",
        "C1b B2b U1 V1",
        "C2ab F1ba U2 V2",
        "F2ba F0ba G1ba G2ba",
        "H2ba H1ba G0ba H0ba",
    ],
}


def kernel(
    nx,
    nz,
    d_early,
    r_early,
    d_count,
    r_count,
    order,
    tok_hbm,
    ids_ref,
    slot_ref,
    weight_ref,
    gate_hbm,
    up_hbm,
    down_hbm,
    out_ref,
    tokx,
    w1,
    wd,
    metas,
    pk,
    wt,
    zb,
    sel,
    xb,
    acc,
    hid,
    po,
    cr,
    ts,
    tr,
    ys,
    rb,
    zs,
    zr,
    last_out,
    last_in,
    w_sem,
    tok_sem,
    e_send,
    e_recv,
    last_send,
    last_recv,
    meta_send,
    meta_recv,
    zb_send,
    zb_recv,
    sel_send,
    sel_recv,
    sx_recv,
    cx_send,
    cx_recv,
    t_send,
    t_recv,
    c1_send,
    c1_recv,
    c2_send,
    c2_recv,
    ce_send,
    ce_recv,
    tt_send,
    tt_recv,
    r_send,
    r_recv,
    zr_send,
    zr_recv,
):
    expert = lax.axis_index("expert")
    tensor = lax.axis_index("tensor")
    z = lax.rem(expert, nz)
    yh = lax.rem(expert // nz, 2)
    x = expert // (2 * nz)
    c = lax.rem(tensor, 2)
    yl = tensor // 2
    half = nz // 2
    tok, width = tok_hbm.shape
    def split(count, early):
        full = width + early
        cuts = [full * i // (128 * count) * 128 for i in range(count)]
        whole = [pl.ds(a, b - a) for a, b in zip(cuts, cuts[1:] + [full])]
        owns = [pl.ds(a, b - a) for a, b in zip(cuts, cuts[1:] + [width])]
        starts = [early] + cuts[1:]
        lates = [pl.ds(a, b - a) for a, b in zip(starts, cuts[1:] + [width])]
        sent = [pl.ds(late.start - early, late.size) for late in lates]
        return whole, owns, lates, sent

    d_whole, d_owns, d_lates, _ = split(d_count, d_early)
    r_whole, r_owns, r_lates, r_sent = split(r_count, r_early)
    extra = pl.ds(width, d_early)
    head = pl.ds(0, d_early)
    r_extra = pl.ds(width, r_early)
    r_head = pl.ds(0, r_early)

    def side(piece, count):
        return piece * 2 // count

    hidden = hid.shape[1]
    own_q = tensor
    far_q = (1 - yl) * 2 + c

    def at_z(d):
        return (expert - z + lax.rem(z + d + nz, nz), tensor)

    def at_plane(xx, rel):
        if rel == 0:
            return ((xx * 2 + yh) * nz + z, tensor)
        return ((xx * 2 + 1 - yh) * nz + z, (1 - yl) * 2 + c)

    t_peer = (expert, far_q)
    c_peer = (expert, yl * 2 + 1 - c)

    def blocks(s):
        if s == 0:
            return 0, 1
        if s == half:
            return nz - 1, 1
        return 2 * s - 1, 2

    def remote(src, dst, send, recv, dev):
        return pltpu.make_async_remote_copy(
            src_ref=src,
            dst_ref=dst,
            send_sem=send,
            recv_sem=recv,
            device_id=dev,
            device_id_type=MESH,
        )

    def wait_bytes(ref, sem):
        pltpu.make_async_copy(ref, ref, sem).wait()

    tok_load = pltpu.make_async_copy(tok_hbm, tokx.at[:, pl.ds(0, width)], tok_sem)
    tok_load.start()
    loads = []
    for q in range(4):
        rows = pl.ds(q * width, width)
        loads.append(
            pltpu.make_async_copy(
                gate_hbm.at[0, rows, :], w1.at[q, :, pl.ds(0, hidden)], w_sem.at[q]
            )
        )
        loads.append(
            pltpu.make_async_copy(
                up_hbm.at[0, rows, :], w1.at[q, :, pl.ds(hidden, hidden)], w_sem.at[4 + q]
            )
        )
        loads.append(
            pltpu.make_async_copy(down_hbm.at[0, :, rows], wd.at[q], w_sem.at[8 + q])
        )
    for load in loads:
        load.start()

    barrier = pltpu.get_barrier_semaphore()
    peers = [at_z(d) for d in range(1, nz)]
    peers += [at_plane(lax.rem(x + d, nx), 0) for d in range(1, nx)]
    peers += [at_plane(lax.rem(x + d, nx), 1) for d in range(nx)]
    peers += [t_peer, c_peer]
    for peer in peers:
        pl.semaphore_signal(barrier, inc=1, device_id=peer, device_id_type=MESH)

    metas[0, pl.ds(0, 8), :] = jnp.where(
        slot_ref[...] >= 0, ids_ref[...] * CAP + slot_ref[...], -1
    )
    metas[0, pl.ds(8, 8), :] = weight_ref[...]

    def delta(b):
        if b == 0:
            return 0
        if b == nz - 1:
            return half
        return (b + 1) // 2 if b % 2 == 1 else nz - b // 2

    seat = 2 * nx * CAP
    per_rel = nx * CAP

    def seat_codes():
        j = lax.broadcasted_iota(jnp.int32, (seat, tok), 0)
        rel = j // per_rel
        rest = j - rel * per_rel
        xe = rest // CAP
        slot = rest - xe * CAP
        far = yh + rel - 2 * yh * rel
        return ((xe * 2 + far) * nz + z) * CAP + slot

    def z_copy(s, way, piece):
        src = tokx if s == 1 else zb.at[2 * s - 3 + way]
        dst = zb.at[nz - 1] if s == half else zb.at[2 * s - 1 + way]
        cols = d_whole[piece]
        i = 2 * s + way
        return remote(
            src.at[:, cols], dst.at[:, cols], zb_send, zb_recv.at[i, piece], at_z(1 - 2 * way)
        )

    def z_parts(s, piece):
        return [z_copy(s, way, piece) for way in range(2) if s < half or way == side(piece, d_count)]

    def z_send(s, piece):
        start_all(z_parts(s, piece))

    def start_all(copies):
        for copy in copies:
            copy.start()

    def routing(b):
        code = seat_codes()
        pick = jnp.zeros((seat, tok), F32)
        high = jnp.zeros((seat, tok), F32)
        low = jnp.zeros((seat, tok), F32)
        for k in range(8):
            hit = metas[delta(b), pl.ds(k, 1), :] == code
            weight = metas[delta(b), pl.ds(8 + k, 1), :]
            top = weight // 128
            pick = jnp.where(hit, 1.0, pick)
            high = jnp.where(hit, top.astype(F32) / 256.0, high)
            low = jnp.where(hit, (weight - top * 128).astype(F32) / 32768.0, low)
        pk[b] = pick.astype(BF16)
        wt[b, :, pl.ds(0, seat)] = high.T.astype(BF16)
        wt[b, :, pl.ds(seat, seat)] = low.T.astype(BF16)

    def pick_rows(b, cols):
        src = tokx[:, cols] if b == 0 else zb[b, :, cols]
        rows = jnp.dot(pk[b], src, preferred_element_type=F32).astype(BF16)
        sel[0, b, :, cols] = rows[:per_rel]
        sel[1, b, :, cols] = rows[per_rel:]

    mine = pl.ds(pl.multiple_of(x * CAP, CAP), CAP)

    def to_plane(s, cols, quarter, there, send, recv):
        bl = pl.ds(*blocks(s))
        pltpu.make_async_copy(
            sel.at[0, bl, mine, cols], xb.at[quarter, 0, bl, mine, there], recv(0)
        ).start()
        for rel in range(2):
            for d in range(1 - rel, nx):
                xx = lax.rem(x + d, nx)
                theirs = pl.ds(pl.multiple_of(xx * CAP, CAP), CAP)
                remote(
                    sel.at[rel, bl, theirs, cols],
                    xb.at[quarter, rel, bl, mine, there],
                    send(rel),
                    recv(rel),
                    at_plane(xx, rel),
                ).start()

    def send_piece(s, piece):
        cols = d_owns[piece]
        to_plane(
            s, cols, own_q, cols, lambda r: sel_send.at[r], lambda r: sel_recv.at[s, r, piece]
        )
        if piece == d_count - 1:
            to_plane(s, extra, far_q, head, lambda r: sel_send.at[r], lambda r: sx_recv.at[s, r])

    routing(0)
    tok_load.wait()
    pick_rows(0, d_whole[0])
    pl.semaphore_wait(barrier, len(peers))

    e_copy = remote(tokx.at[:, head], tokx.at[:, extra], e_send, e_recv, t_peer)
    start_all([e_copy])
    z_send(1, 0)
    send_piece(0, 0)
    for d in range(1, nz):
        remote(metas.at[0], metas.at[d], meta_send, meta_recv, at_z(d)).start()
    for piece in range(1, d_count):
        if piece == d_count - 1:
            e_copy.wait_recv()
        z_send(1, piece)
        pick_rows(0, d_whole[piece])
        send_piece(0, piece)

    state = {"meta": False}

    def stage_a(s, piece):
        first, count = blocks(s)
        for copy in z_parts(s, piece):
            copy.wait_recv()
        if s < half:
            z_send(s + 1, piece)
        if not state["meta"]:
            wait_bytes(metas.at[pl.ds(1, nz - 1)], meta_recv)
            state["meta"] = True
        for b in range(first, first + count):
            if piece == 0:
                routing(b)
            pick_rows(b, d_whole[piece])
        send_piece(s, piece)

    def t_copies(s, piece):
        bl = pl.ds(*blocks(s))
        out = []
        for rel in range(2):
            ref = xb.at[own_q if rel == 0 else far_q, rel, bl, :, d_lates[piece]]
            out.append(remote(ref, ref, t_send, t_recv.at[s, rel, piece], t_peer))
        return out

    def c_copies(s, piece, part):
        bl = pl.ds(*blocks(s))
        send, recv = ((c1_send, c1_recv), (cx_send, cx_recv), (c2_send, c2_recv))[part]
        cols = (d_owns[piece], head, d_lates[piece])[part]
        out = []
        for rel in range(2):
            ref = xb.at[own_q if (rel == 0) == (part == 0) else far_q, rel, bl, :, cols]
            i = (s, rel) if part == 1 else (s, rel, piece)
            out.append(remote(ref, ref, send, recv.at[i], c_peer))
        return out

    def stage_b(s, piece):
        bl = pl.ds(*blocks(s))
        t_list, c_list = t_copies(s, piece), c_copies(s, piece, 0)
        for rel in range(2):
            got = xb.at[own_q if rel == 0 else far_q, rel, bl, :, d_owns[piece]]
            wait_bytes(got, sel_recv.at[s, rel, piece])
            start_all([t_list[rel], c_list[rel]])
        if piece == d_count - 1:
            x_list = c_copies(s, piece, 1)
            for rel in range(2):
                got = xb.at[far_q if rel == 0 else own_q, rel, bl, :, head]
                wait_bytes(got, sx_recv.at[s, rel])
                start_all([x_list[rel]])

    def stage_c(s, piece):
        t_list, c_list = t_copies(s, piece), c_copies(s, piece, 2)
        for rel in range(2):
            t_list[rel].wait_recv()
            start_all([c_list[rel]])

    def ce_copies(s):
        bl = pl.ds(*blocks(s))
        return [
            remote(
                po.at[2 * p + 1 - c, :, bl],
                cr.at[p, :, bl],
                ce_send,
                ce_recv.at[s, p],
                c_peer,
            )
            for p in range(2)
        ]

    loaded = {"w1": False, "wd": False}

    def stage_u(s):
        first, count = blocks(s)
        bl = pl.ds(first, count)
        rows = count * seat
        for part in range(3):
            for piece in range(d_count):
                if part != 1 or piece == d_count - 1:
                    for copy in c_copies(s, piece, part):
                        copy.wait_recv()
        if not loaded["w1"]:
            loaded["w1"] = True
            for load in loads:
                load.wait()

        xs = jnp.concatenate([xb[q, :, bl].reshape(rows, width) for q in range(4)], axis=1)
        ws = jnp.concatenate([w1[q] for q in range(4)], axis=0)
        acc[pl.ds(0, rows), :] = jnp.dot(xs, ws, preferred_element_type=F32)
        gate = acc[pl.ds(0, rows), pl.ds(0, hidden)]
        up = acc[pl.ds(0, rows), pl.ds(hidden, hidden)]
        hid[pl.ds(0, rows), :] = (gate / (1.0 + jnp.exp(-gate)) * up).astype(BF16)

    def stage_v(s):
        first, count = blocks(s)
        bl = pl.ds(first, count)
        rows = count * seat

        copies = ce_copies(s)
        for core in (1 - c, c):
            for p in range(2):
                q = 2 * p + core
                part = jnp.dot(hid[pl.ds(0, rows), :], wd[q], preferred_element_type=F32)
                po[q, :, bl] = part.astype(BF16).reshape(2, count, per_rel, width)
                start_all(copies[p : p + 1])
            copies = []

    def tt_copies(s, piece):
        bl = pl.ds(*blocks(s))
        cols = r_sent[piece]
        return [
            remote(
                ts.at[rel, bl, :, cols],
                tr.at[rel, bl, :, cols],
                tt_send,
                tt_recv.at[s, rel, piece],
                t_peer,
            )
            for rel in range(2)
        ]

    def cores(p, rel, bl, cols):
        ours = po[2 * p + c, rel, bl, :, cols].astype(F32)
        return ours + cr[p, rel, bl, :, cols].astype(F32)

    def stage_f(s, piece):
        bl = pl.ds(*blocks(s))
        copies = tt_copies(s, piece)
        if piece == r_count - 1:
            for copy in ce_copies(s):
                copy.wait_recv()
        for rel in range(2):
            p = 1 - yl if rel == 0 else yl
            ts[rel, bl, :, r_sent[piece]] = cores(p, rel, bl, r_lates[piece]).astype(BF16)
            start_all([copies[rel]])

    def stage_g(s, piece):
        bl = pl.ds(*blocks(s))
        copies = tt_copies(s, piece)
        cols = r_whole[piece]
        for rel in range(2):
            p = yl if rel == 0 else 1 - yl
            if piece == 0:
                ys[rel, bl, :, r_head] = cores(p, rel, bl, r_head).astype(BF16)
            elif piece == r_count - 1:
                ys[rel, bl, :, r_extra] = cores(1 - p, rel, bl, r_head).astype(BF16)
            copies[rel].wait_recv()
            total = cores(p, rel, bl, r_lates[piece]) + tr[rel, bl, :, r_sent[piece]].astype(F32)
            ys[rel, bl, :, r_lates[piece]] = total.astype(BF16)
            if rel == 0:
                pltpu.make_async_copy(
                    ys.at[0, bl, mine, cols], rb.at[0, bl, mine, cols], r_recv.at[s, 0, piece]
                ).start()
            for d in range(1 - rel, nx):
                xx = lax.rem(x + d, nx)
                theirs = pl.ds(pl.multiple_of(xx * CAP, CAP), CAP)
                remote(
                    ys.at[rel, bl, theirs, cols],
                    rb.at[rel, bl, mine, cols],
                    r_send.at[rel],
                    r_recv.at[s, rel, piece],
                    at_plane(xx, rel),
                ).start()
    def back_copy(s, way, piece):
        b = nz - 1 if s == half else 2 * s - 1 + way
        cols = r_whole[piece]
        i = 2 * s + way
        return remote(
            zs.at[b, :, cols], zr.at[b, :, cols], zr_send, zr_recv.at[i, piece], at_z(2 * way - 1)
        )

    last = remote(last_out, last_in, last_send, last_recv, t_peer)

    def stage_h(s, piece):
        first, count = blocks(s)
        cols = r_whole[piece]
        for rel in range(2):
            wait_bytes(rb.at[rel, pl.ds(first, count), :, cols], r_recv.at[s, rel, piece])
        for b in range(first, first + count):
            near, far = rb[0, b, :, cols], rb[1, b, :, cols]
            rows = jnp.concatenate([near, far, near, far], axis=0)
            total = jnp.dot(wt[b], rows, preferred_element_type=F32)
            for way in range(2) if s == 0 else (b - first,):
                if s == half or (s + 1 == half and way != side(piece, r_count)):
                    continue
                back_copy(s + 1, way, piece).wait_recv()
                src = nz - 1 if s + 1 == half else 2 * s + 1 + way
                total += zr[src, :, cols].astype(F32)
            if s > 0:
                zs[b, :, cols] = total.astype(BF16)
                start_all([back_copy(s, side(piece, r_count) if s == half else b - first, piece)])
            elif piece == r_count - 1:
                mid = r_owns[piece].size
                last_out[...] = total[:, mid:].astype(BF16)
                start_all([last])
                out_ref[:, r_owns[piece]] = total[:, :mid].astype(BF16)
            elif piece > 0:
                out_ref[:, cols] = total.astype(BF16)
            else:
                out_ref[:, r_lates[0]] = total[:, r_early:].astype(BF16)
                last.wait_recv()
                out_ref[:, r_head] = (total[:, :r_early] + last_in[...].astype(F32)).astype(BF16)

    stages = {
        "A": stage_a,
        "B": stage_b,
        "C": stage_c,
        "U": stage_u,
        "V": stage_v,
        "F": stage_f,
        "G": stage_g,
        "H": stage_h,
    }
    for name, *step in order:
        stages[name](*step)
    some = pl.ds(0, per_rel - CAP)
    e_copy.wait_send()
    last.wait_send()
    wait_bytes(metas.at[pl.ds(1, nz - 1)], meta_send)
    wait_bytes(zb.at[pl.ds(0, nz - 1)], zb_send)
    wait_bytes(zs.at[pl.ds(0, nz - 1)], zr_send)
    for ref, sem in ((sel, sel_send), (ys, r_send)):
        wait_bytes(ref.at[0, :, some, :], sem.at[0])
        wait_bytes(ref.at[1], sem.at[1])
    late = xb.at[0, :, :, :, pl.ds(d_early, width - d_early)]
    wait_bytes(late, t_send)
    wait_bytes(late, c2_send)
    wait_bytes(ts, tt_send)
    wait_bytes(xb.at[0], c1_send)
    wait_bytes(xb.at[0, :, :, :, head], cx_send)
    wait_bytes(cr, ce_send)


def make_order(half):
    order = []
    for word in " ".join(ORDERS[half]).split():
        step = (word[0], int(word[1]))
        for piece in word[2:]:
            order.append(step + ("abcdef".index(piece),))
        if len(word) == 2:
            order.append(step)
    return order


def moe(nx, nz, d_early, r_early, tokens, ids, slots, weights, gate_weight, up_weight, down_weight):
    tok, width = tokens.shape
    hidden = gate_weight.shape[2]
    half = nz // 2
    chunks = half + 1
    per_rel = nx * CAP
    rows = 4 * per_rel
    dma = pltpu.SemaphoreType.DMA
    d_full, r_full = width + d_early, width + r_early
    vmem = pl.BlockSpec(memory_space=pltpu.VMEM)
    hbm = pl.BlockSpec(memory_space=pl.ANY)
    scratch = [
        pltpu.VMEM((tok, d_full), BF16),
        pltpu.VMEM((4, width, 2 * hidden), BF16),
        pltpu.VMEM((4, hidden, width), BF16),
        pltpu.VMEM((nz, 16, tok), jnp.int32),
        pltpu.VMEM((nz, 2 * per_rel, tok), BF16),
        pltpu.VMEM((nz, tok, 4 * per_rel), BF16),
        pltpu.VMEM((nz, tok, d_full), BF16),
        pltpu.VMEM((2, nz, per_rel, d_full), BF16),
        pltpu.VMEM((4, 2, nz, per_rel, width), BF16),
        pltpu.VMEM((rows, 2 * hidden), F32),
        pltpu.VMEM((rows, hidden), BF16),
        pltpu.VMEM((4, 2, nz, per_rel, width), BF16),
        pltpu.VMEM((2, 2, nz, per_rel, width), BF16),
        pltpu.VMEM((2, nz, per_rel, width - r_early), BF16),
        pltpu.VMEM((2, nz, per_rel, width - r_early), BF16),
        pltpu.VMEM((2, nz, per_rel, r_full), BF16),
        pltpu.VMEM((2, nz, per_rel, r_full), BF16),
        pltpu.VMEM((nz, tok, r_full), BF16),
        pltpu.VMEM((nz, tok, r_full), BF16),
        pltpu.VMEM((tok, r_early), BF16),
        pltpu.VMEM((tok, r_early), BF16),
        dma((12,)),
        dma,
        dma,
        dma,
        dma,
        dma,
        dma,
        dma,
        dma,
        dma((2 * chunks, D_COUNT)),
        dma((2,)),
        dma((chunks, 2, D_COUNT)),
        dma((chunks, 2)),
        dma,
        dma((chunks, 2)),
        dma,
        dma((chunks, 2, D_COUNT)),
        dma,
        dma((chunks, 2, D_COUNT)),
        dma,
        dma((chunks, 2, D_COUNT)),
        dma,
        dma((chunks, 2)),
        dma,
        dma((chunks, 2, R_COUNT)),
        dma((2,)),
        dma((chunks, 2, R_COUNT)),
        dma,
        dma((2 * chunks, R_COUNT)),
    ]
    return pl.pallas_call(
        functools.partial(kernel, nx, nz, d_early, r_early, D_COUNT, R_COUNT, make_order(half)),
        out_shape=pltpu.VMEM((tok, width), BF16),
        in_specs=[hbm, vmem, vmem, vmem, hbm, hbm, hbm],
        out_specs=vmem,
        scratch_shapes=scratch,
        compiler_params=pltpu.CompilerParams(
            collective_id=0,
            has_side_effects=True,
            vmem_limit_bytes=60 * 1024 * 1024,
        ),
    )(tokens, ids, slots, weights, gate_weight, up_weight, down_weight)


def shards(nx, nz, d_early, r_early, tokens, expert_ids, slot_index, gate_fixed, *expert_weights):
    routing = (expert_ids.T, slot_index.T, gate_fixed.T)
    return moe(nx, nz, d_early, r_early, tokens, *routing, *expert_weights)


def solution(mesh, nx=4, nz=8, d_early=128, r_early=256):
    in_specs = (
        P("expert", "tensor"),
        P("expert", None),
        P("expert", None),
        P("expert", None),
        P("expert", None, "tensor"),
        P("expert", None, "tensor"),
        P("expert", "tensor", None),
    )
    return jax.shard_map(
        functools.partial(shards, nx, nz, d_early, r_early),
        mesh=mesh,
        in_specs=in_specs,
        out_specs=P("expert", "tensor"),
        check_vma=False,
    )
```

```python
import functools

import jax
import jax.numpy as jnp
from jax import lax
from jax.experimental import pallas as pl
from jax.experimental.pallas import tpu as pltpu
from jax.sharding import PartitionSpec as P

CAP = 16
MESH = pl.DeviceIdType.MESH
BF16 = jnp.bfloat16
F32 = jnp.float32


D_COUNT = 2
ORDERS = {
    4: [
        "B0ab A1a C0ab A1b",
        "B1a U0 V0 A2a",
        "B1b A2b C1a B2a",
        "C1b A3a B2b U1",
        "A3b V1 B3a C2a",
        "B3b C2b A4ab U2",
        "V2 B4a C3a B4b",
        "C3b U3 V3 C4ab",
        "F3ba G3c U4 V4",
        "F4ba G4c F2ba G2c",
        "G3b G3a H4c G4b",
        "G4a F1ba G1c H3c",
        "H4b H4a H3b H3a",
        "G2b G2a F0ba G0c",
        "H2c H2b H2a G1b",
        "H1c G1a H1b H1a",
        "H0c G0b G0a H0b",
        "H0a L0",
    ],
    1: [
        "B0ab A1ab B1ab C0ab",
        "U0 V0 C1ab U1",
        "V1 F0ba G0c F1ba",
        "G1c G1ba H1cba G0ba",
        "H0cba L0",
    ],
    2: [
        "B0ab A1a C0ab A1b",
        "B1a U0 V0 A2a",
        "B1b A2b C1a B2a",
        "C1b B2b U1 V1",
        "C2ab F1ba G1c U2",
        "V2 F2ba G2c F0ba",
        "G0c G1ba G2ba H2cba",
        "H1cba G0ba H0cba L0",
    ],
}


def kernel(
    nx,
    nz,
    d_early,
    r_early,
    d_count,
    order,
    tok_hbm,
    ids_ref,
    slot_ref,
    weight_ref,
    gate_hbm,
    up_hbm,
    down_hbm,
    out_ref,
    tokx,
    w1,
    wd,
    metas,
    pk,
    wt,
    zb,
    sel,
    xb,
    acc,
    hid,
    po,
    cr,
    ts,
    tr,
    ys,
    rb,
    zs,
    zr,
    last_out,
    last_in,
    w_sem,
    tok_sem,
    e_send,
    e_recv,
    last_send,
    last_recv,
    meta_send,
    meta_recv,
    zb_send,
    zb_recv,
    sel_send,
    sel_recv,
    sx_recv,
    cx_send,
    cx_recv,
    t_send,
    t_recv,
    c1_send,
    c1_recv,
    c2_send,
    c2_recv,
    ce_send,
    ce_recv,
    tt_send,
    tt_recv,
    r_send,
    r_recv,
    zr_send,
    zr_recv,
):
    expert = lax.axis_index("expert")
    tensor = lax.axis_index("tensor")
    z = lax.rem(expert, nz)
    yh = lax.rem(expert // nz, 2)
    x = expert // (2 * nz)
    c = lax.rem(tensor, 2)
    yl = tensor // 2
    half = nz // 2
    tok, width = tok_hbm.shape
    def split(count, early):
        full = width + early
        cuts = [full * i // (128 * count) * 128 for i in range(count)]
        whole = [pl.ds(a, b - a) for a, b in zip(cuts, cuts[1:] + [full])]
        owns = [pl.ds(a, b - a) for a, b in zip(cuts, cuts[1:] + [width])]
        starts = [early] + cuts[1:]
        lates = [pl.ds(a, b - a) for a, b in zip(starts, cuts[1:] + [width])]
        return whole, owns, lates

    d_whole, d_owns, d_lates = split(d_count, d_early)
    late = width - r_early
    mid = late // 256 * 128
    r_count = 3
    r_whole = (pl.ds(0, mid), pl.ds(mid, late - mid), pl.ds(late, 2 * r_early))
    r_lates = (pl.ds(r_early, mid), pl.ds(r_early + mid, late - mid))
    extra = pl.ds(width, d_early)
    head = pl.ds(0, d_early)
    r_head = pl.ds(0, r_early)

    def side(piece, count):
        return piece * 2 // count

    hidden = hid.shape[1]
    own_q = tensor
    far_q = (1 - yl) * 2 + c

    def at_z(d):
        return (expert - z + lax.rem(z + d + nz, nz), tensor)

    def at_plane(xx, rel):
        if rel == 0:
            return ((xx * 2 + yh) * nz + z, tensor)
        return ((xx * 2 + 1 - yh) * nz + z, (1 - yl) * 2 + c)

    t_peer = (expert, far_q)
    c_peer = (expert, yl * 2 + 1 - c)

    def blocks(s):
        if s == 0:
            return 0, 1
        if s == half:
            return nz - 1, 1
        return 2 * s - 1, 2

    def remote(src, dst, send, recv, dev):
        return pltpu.make_async_remote_copy(
            src_ref=src,
            dst_ref=dst,
            send_sem=send,
            recv_sem=recv,
            device_id=dev,
            device_id_type=MESH,
        )

    def wait_bytes(ref, sem):
        pltpu.make_async_copy(ref, ref, sem).wait()

    tok_load = pltpu.make_async_copy(tok_hbm, tokx.at[:, pl.ds(0, width)], tok_sem)
    tok_load.start()
    loads = []
    for q in range(4):
        rows = pl.ds(q * width, width)
        loads.append(
            pltpu.make_async_copy(
                gate_hbm.at[0, rows, :], w1.at[q, :, pl.ds(0, hidden)], w_sem.at[q]
            )
        )
        loads.append(
            pltpu.make_async_copy(
                up_hbm.at[0, rows, :], w1.at[q, :, pl.ds(hidden, hidden)], w_sem.at[4 + q]
            )
        )
        loads.append(
            pltpu.make_async_copy(down_hbm.at[0, :, rows], wd.at[q], w_sem.at[8 + q])
        )
    for load in loads:
        load.start()

    barrier = pltpu.get_barrier_semaphore()
    peers = [at_z(d) for d in range(1, nz)]
    peers += [at_plane(lax.rem(x + d, nx), 0) for d in range(1, nx)]
    peers += [at_plane(lax.rem(x + d, nx), 1) for d in range(nx)]
    peers += [t_peer, c_peer]
    for peer in peers:
        pl.semaphore_signal(barrier, inc=1, device_id=peer, device_id_type=MESH)

    metas[0, pl.ds(0, 8), :] = jnp.where(
        slot_ref[...] >= 0, ids_ref[...] * CAP + slot_ref[...], -1
    )
    metas[0, pl.ds(8, 8), :] = weight_ref[...]

    def delta(b):
        if b == 0:
            return 0
        if b == nz - 1:
            return half
        return (b + 1) // 2 if b % 2 == 1 else nz - b // 2

    seat = 2 * nx * CAP
    per_rel = nx * CAP

    def seat_codes():
        j = lax.broadcasted_iota(jnp.int32, (seat, tok), 0)
        rel = j // per_rel
        rest = j - rel * per_rel
        xe = rest // CAP
        slot = rest - xe * CAP
        far = yh + rel - 2 * yh * rel
        return ((xe * 2 + far) * nz + z) * CAP + slot

    def meta_copy(d):
        return remote(metas.at[0], metas.at[d], meta_send, meta_recv.at[d], at_z(d))

    def z_copy(s, way, piece):
        src = tokx if s == 1 else zb.at[2 * s - 3 + way]
        dst = zb.at[nz - 1] if s == half else zb.at[2 * s - 1 + way]
        cols = d_whole[piece]
        i = 2 * s + way
        return remote(
            src.at[:, cols], dst.at[:, cols], zb_send, zb_recv.at[i, piece], at_z(1 - 2 * way)
        )

    def z_parts(s, piece):
        return [z_copy(s, way, piece) for way in range(2) if s < half or way == side(piece, d_count)]

    def z_send(s, piece):
        start_all(z_parts(s, piece))

    def start_all(copies):
        for copy in copies:
            copy.start()

    def routing(b):
        code = seat_codes()
        pick = jnp.zeros((seat, tok), F32)
        high = jnp.zeros((seat, tok), F32)
        low = jnp.zeros((seat, tok), F32)
        for k in range(8):
            hit = metas[delta(b), pl.ds(k, 1), :] == code
            weight = metas[delta(b), pl.ds(8 + k, 1), :]
            top = weight // 128
            pick = jnp.where(hit, 1.0, pick)
            high = jnp.where(hit, top.astype(F32) / 256.0, high)
            low = jnp.where(hit, (weight - top * 128).astype(F32) / 32768.0, low)
        pk[b] = pick.astype(BF16)
        wt[b, :, pl.ds(0, seat)] = high.T.astype(BF16)
        wt[b, :, pl.ds(seat, seat)] = low.T.astype(BF16)

    def pick_rows(b, cols):
        src = tokx[:, cols] if b == 0 else zb[b, :, cols]
        rows = jnp.dot(pk[b], src, preferred_element_type=F32).astype(BF16)
        sel[0, b, :, cols] = rows[:per_rel]
        sel[1, b, :, cols] = rows[per_rel:]

    mine = pl.ds(pl.multiple_of(x * CAP, CAP), CAP)

    def to_plane(s, cols, quarter, there, send, recv):
        bl = pl.ds(*blocks(s))
        pltpu.make_async_copy(
            sel.at[0, bl, mine, cols], xb.at[quarter, 0, bl, mine, there], recv(0)
        ).start()
        for rel in range(2):
            for d in range(1 - rel, nx):
                xx = lax.rem(x + d, nx)
                theirs = pl.ds(pl.multiple_of(xx * CAP, CAP), CAP)
                remote(
                    sel.at[rel, bl, theirs, cols],
                    xb.at[quarter, rel, bl, mine, there],
                    send(rel),
                    recv(rel),
                    at_plane(xx, rel),
                ).start()

    def send_piece(s, piece):
        cols = d_owns[piece]
        to_plane(
            s, cols, own_q, cols, lambda r: sel_send.at[r], lambda r: sel_recv.at[s, r, piece]
        )
        if piece == d_count - 1:
            to_plane(s, extra, far_q, head, lambda r: sel_send.at[r], lambda r: sx_recv.at[s, r])

    routing(0)
    tok_load.wait()
    pick_rows(0, d_whole[0])
    pl.semaphore_wait(barrier, len(peers))

    e_copy = remote(tokx.at[:, head], tokx.at[:, extra], e_send, e_recv, t_peer)
    start_all([e_copy])
    z_send(1, 0)
    send_piece(0, 0)
    for d in range(1, nz):
        meta_copy(d).start()
    for piece in range(1, d_count):
        if piece == d_count - 1:
            e_copy.wait_recv()
        z_send(1, piece)
        pick_rows(0, d_whole[piece])
        send_piece(0, piece)

    def stage_a(s, piece):
        first, count = blocks(s)
        for copy in z_parts(s, piece):
            copy.wait_recv()
        if s < half:
            z_send(s + 1, piece)
        for b in range(first, first + count):
            if piece == 0:
                meta_copy(delta(b)).wait_recv()
                routing(b)
            pick_rows(b, d_whole[piece])
        send_piece(s, piece)

    def t_copies(s, piece):
        bl = pl.ds(*blocks(s))
        out = []
        for rel in range(2):
            ref = xb.at[own_q if rel == 0 else far_q, rel, bl, :, d_lates[piece]]
            out.append(remote(ref, ref, t_send, t_recv.at[s, rel, piece], t_peer))
        return out

    def c_copies(s, piece, part):
        bl = pl.ds(*blocks(s))
        send, recv = ((c1_send, c1_recv), (cx_send, cx_recv), (c2_send, c2_recv))[part]
        cols = (d_owns[piece], head, d_lates[piece])[part]
        out = []
        for rel in range(2):
            ref = xb.at[own_q if (rel == 0) == (part == 0) else far_q, rel, bl, :, cols]
            i = (s, rel) if part == 1 else (s, rel, piece)
            out.append(remote(ref, ref, send, recv.at[i], c_peer))
        return out

    def stage_b(s, piece):
        bl = pl.ds(*blocks(s))
        t_list, c_list = t_copies(s, piece), c_copies(s, piece, 0)
        for rel in range(2):
            got = xb.at[own_q if rel == 0 else far_q, rel, bl, :, d_owns[piece]]
            wait_bytes(got, sel_recv.at[s, rel, piece])
            start_all([t_list[rel], c_list[rel]])
        if piece == d_count - 1:
            x_list = c_copies(s, piece, 1)
            for rel in range(2):
                got = xb.at[far_q if rel == 0 else own_q, rel, bl, :, head]
                wait_bytes(got, sx_recv.at[s, rel])
                start_all([x_list[rel]])

    def stage_c(s, piece):
        t_list, c_list = t_copies(s, piece), c_copies(s, piece, 2)
        for rel in range(2):
            t_list[rel].wait_recv()
            start_all([c_list[rel]])

    def ce_copies(s):
        bl = pl.ds(*blocks(s))
        return [
            remote(
                po.at[2 * p + 1 - c, :, bl],
                cr.at[p, :, bl],
                ce_send,
                ce_recv.at[s, p],
                c_peer,
            )
            for p in range(2)
        ]

    loaded = {"w1": False, "wd": False}

    def stage_u(s):
        first, count = blocks(s)
        bl = pl.ds(first, count)
        rows = count * seat
        for part in range(3):
            for piece in range(d_count):
                if part != 1 or piece == d_count - 1:
                    for copy in c_copies(s, piece, part):
                        copy.wait_recv()
        if not loaded["w1"]:
            loaded["w1"] = True
            for load in loads:
                load.wait()

        xs = jnp.concatenate([xb[q, :, bl].reshape(rows, width) for q in range(4)], axis=1)
        ws = jnp.concatenate([w1[q] for q in range(4)], axis=0)
        acc[pl.ds(0, rows), :] = jnp.dot(xs, ws, preferred_element_type=F32)
        gate = acc[pl.ds(0, rows), pl.ds(0, hidden)]
        up = acc[pl.ds(0, rows), pl.ds(hidden, hidden)]
        hid[pl.ds(0, rows), :] = (gate / (1.0 + jnp.exp(-gate)) * up).astype(BF16)

    def stage_v(s):
        first, count = blocks(s)
        bl = pl.ds(first, count)
        rows = count * seat

        copies = ce_copies(s)
        for core in (1 - c, c):
            for p in range(2):
                q = 2 * p + core
                part = jnp.dot(hid[pl.ds(0, rows), :], wd[q], preferred_element_type=F32)
                po[q, :, bl] = part.astype(BF16).reshape(2, count, per_rel, width)
                start_all(copies[p : p + 1])
            copies = []

    def tt_copies(s, piece):
        bl = pl.ds(*blocks(s))
        cols = r_whole[piece]
        return [
            remote(
                ts.at[rel, bl, :, cols],
                tr.at[rel, bl, :, cols],
                tt_send,
                tt_recv.at[s, rel, piece],
                t_peer,
            )
            for rel in range(2)
        ]

    def cores(p, rel, bl, cols):
        ours = po[2 * p + c, rel, bl, :, cols].astype(F32)
        return ours + cr[p, rel, bl, :, cols].astype(F32)

    def stage_f(s, piece):
        bl = pl.ds(*blocks(s))
        copies = tt_copies(s, piece)
        if piece == 1:
            for copy in ce_copies(s):
                copy.wait_recv()
        for rel in range(2):
            p = 1 - yl if rel == 0 else yl
            ts[rel, bl, :, r_whole[piece]] = cores(p, rel, bl, r_lates[piece]).astype(BF16)
            start_all([copies[rel]])

    def stage_g(s, piece):
        bl = pl.ds(*blocks(s))
        copies = tt_copies(s, piece) if piece < 2 else None
        cols = r_whole[piece]
        for rel in range(2):
            p = yl if rel == 0 else 1 - yl
            if piece == 2:
                ys[rel, bl, :, pl.ds(late, r_early)] = cores(p, rel, bl, r_head).astype(BF16)
                ys[rel, bl, :, pl.ds(width, r_early)] = cores(1 - p, rel, bl, r_head).astype(BF16)
            else:
                copies[rel].wait_recv()
                total = cores(p, rel, bl, r_lates[piece]) + tr[rel, bl, :, cols].astype(F32)
                ys[rel, bl, :, cols] = total.astype(BF16)
            if rel == 0:
                pltpu.make_async_copy(
                    ys.at[0, bl, mine, cols], rb.at[0, bl, mine, cols], r_recv.at[s, 0, piece]
                ).start()
            for d in range(1 - rel, nx):
                xx = lax.rem(x + d, nx)
                theirs = pl.ds(pl.multiple_of(xx * CAP, CAP), CAP)
                remote(
                    ys.at[rel, bl, theirs, cols],
                    rb.at[rel, bl, mine, cols],
                    r_send.at[rel],
                    r_recv.at[s, rel, piece],
                    at_plane(xx, rel),
                ).start()
    def back_copy(s, way, piece):
        b = nz - 1 if s == half else 2 * s - 1 + way
        cols = r_whole[piece]
        i = 2 * s + way
        return remote(
            zs.at[b, :, cols], zr.at[b, :, cols], zr_send, zr_recv.at[i, piece], at_z(2 * way - 1)
        )

    last = remote(last_out, last_in, last_send, last_recv, t_peer)

    def stage_h(s, piece):
        first, count = blocks(s)
        cols = r_whole[piece]
        for rel in range(2):
            wait_bytes(rb.at[rel, pl.ds(first, count), :, cols], r_recv.at[s, rel, piece])
        for b in range(first, first + count):
            near, far = rb[0, b, :, cols], rb[1, b, :, cols]
            rows = jnp.concatenate([near, far, near, far], axis=0)
            total = jnp.dot(wt[b], rows, preferred_element_type=F32)
            for way in range(2) if s == 0 else (b - first,):
                if s == half or (s + 1 == half and way != side(piece, r_count)):
                    continue
                back_copy(s + 1, way, piece).wait_recv()
                src = nz - 1 if s + 1 == half else 2 * s + 1 + way
                total += zr[src, :, cols].astype(F32)
            if s > 0:
                zs[b, :, cols] = total.astype(BF16)
                start_all([back_copy(s, side(piece, r_count) if s == half else b - first, piece)])
            elif piece == 2:
                last_out[...] = total[:, r_early:].astype(BF16)
                start_all([last])
                acc[pl.ds(0, tok), r_head] = total[:, :r_early]
            else:
                out_ref[:, r_lates[piece]] = total.astype(BF16)

    def stage_l(s):
        last.wait_recv()
        both = acc[pl.ds(0, tok), r_head] + last_in[...].astype(F32)
        out_ref[:, r_head] = both.astype(BF16)

    stages = {
        "A": stage_a,
        "B": stage_b,
        "C": stage_c,
        "U": stage_u,
        "V": stage_v,
        "F": stage_f,
        "G": stage_g,
        "H": stage_h,
        "L": stage_l,
    }
    for name, *step in order:
        stages[name](*step)
    some = pl.ds(0, per_rel - CAP)
    e_copy.wait_send()
    last.wait_send()
    wait_bytes(metas.at[pl.ds(1, nz - 1)], meta_send)
    wait_bytes(zb.at[pl.ds(0, nz - 1)], zb_send)
    wait_bytes(zs.at[pl.ds(0, nz - 1)], zr_send)
    for ref, sem in ((sel, sel_send), (ys, r_send)):
        wait_bytes(ref.at[0, :, some, :], sem.at[0])
        wait_bytes(ref.at[1], sem.at[1])
    crossed = xb.at[0, :, :, :, pl.ds(d_early, width - d_early)]
    wait_bytes(crossed, t_send)
    wait_bytes(crossed, c2_send)
    wait_bytes(ts, tt_send)
    wait_bytes(xb.at[0], c1_send)
    wait_bytes(xb.at[0, :, :, :, head], cx_send)
    wait_bytes(cr, ce_send)


def make_order(half):
    order = []
    for word in " ".join(ORDERS[half]).split():
        step = (word[0], int(word[1]))
        for piece in word[2:]:
            order.append(step + ("abcdef".index(piece),))
        if len(word) == 2:
            order.append(step)
    return order


def moe(nx, nz, d_early, r_early, tokens, ids, slots, weights, gate_weight, up_weight, down_weight):
    tok, width = tokens.shape
    hidden = gate_weight.shape[2]
    half = nz // 2
    chunks = half + 1
    per_rel = nx * CAP
    rows = 4 * per_rel
    dma = pltpu.SemaphoreType.DMA
    d_full, r_full = width + d_early, width + r_early
    vmem = pl.BlockSpec(memory_space=pltpu.VMEM)
    hbm = pl.BlockSpec(memory_space=pl.ANY)
    scratch = [
        pltpu.VMEM((tok, d_full), BF16),
        pltpu.VMEM((4, width, 2 * hidden), BF16),
        pltpu.VMEM((4, hidden, width), BF16),
        pltpu.VMEM((nz, 16, tok), jnp.int32),
        pltpu.VMEM((nz, 2 * per_rel, tok), BF16),
        pltpu.VMEM((nz, tok, 4 * per_rel), BF16),
        pltpu.VMEM((nz, tok, d_full), BF16),
        pltpu.VMEM((2, nz, per_rel, d_full), BF16),
        pltpu.VMEM((4, 2, nz, per_rel, width), BF16),
        pltpu.VMEM((rows, 2 * hidden), F32),
        pltpu.VMEM((rows, hidden), BF16),
        pltpu.VMEM((4, 2, nz, per_rel, width), BF16),
        pltpu.VMEM((2, 2, nz, per_rel, width), BF16),
        pltpu.VMEM((2, nz, per_rel, width - r_early), BF16),
        pltpu.VMEM((2, nz, per_rel, width - r_early), BF16),
        pltpu.VMEM((2, nz, per_rel, r_full), BF16),
        pltpu.VMEM((2, nz, per_rel, r_full), BF16),
        pltpu.VMEM((nz, tok, r_full), BF16),
        pltpu.VMEM((nz, tok, r_full), BF16),
        pltpu.VMEM((tok, r_early), BF16),
        pltpu.VMEM((tok, r_early), BF16),
        dma((12,)),
        dma,
        dma,
        dma,
        dma,
        dma,
        dma,
        dma((nz,)),
        dma,
        dma((2 * chunks, D_COUNT)),
        dma((2,)),
        dma((chunks, 2, D_COUNT)),
        dma((chunks, 2)),
        dma,
        dma((chunks, 2)),
        dma,
        dma((chunks, 2, D_COUNT)),
        dma,
        dma((chunks, 2, D_COUNT)),
        dma,
        dma((chunks, 2, D_COUNT)),
        dma,
        dma((chunks, 2)),
        dma,
        dma((chunks, 2, 3)),
        dma((2,)),
        dma((chunks, 2, 3)),
        dma,
        dma((2 * chunks, 3)),
    ]
    return pl.pallas_call(
        functools.partial(kernel, nx, nz, d_early, r_early, D_COUNT, make_order(half)),
        out_shape=pltpu.VMEM((tok, width), BF16),
        in_specs=[hbm, vmem, vmem, vmem, hbm, hbm, hbm],
        out_specs=vmem,
        scratch_shapes=scratch,
        compiler_params=pltpu.CompilerParams(
            collective_id=0,
            has_side_effects=True,
            vmem_limit_bytes=60 * 1024 * 1024,
        ),
    )(tokens, ids, slots, weights, gate_weight, up_weight, down_weight)


def shards(nx, nz, d_early, r_early, tokens, expert_ids, slot_index, gate_fixed, *expert_weights):
    routing = (expert_ids.T, slot_index.T, gate_fixed.T)
    return moe(nx, nz, d_early, r_early, tokens, *routing, *expert_weights)


def solution(mesh, nx=4, nz=8, d_early=128, r_early=256):
    in_specs = (
        P("expert", "tensor"),
        P("expert", None),
        P("expert", None),
        P("expert", None),
        P("expert", None, "tensor"),
        P("expert", None, "tensor"),
        P("expert", "tensor", None),
    )
    return jax.shard_map(
        functools.partial(shards, nx, nz, d_early, r_early),
        mesh=mesh,
        in_specs=in_specs,
        out_specs=P("expert", "tensor"),
        check_vma=False,
    )
```

```python
import functools

import jax
import jax.numpy as jnp
from jax import lax
from jax.experimental import pallas as pl
from jax.experimental.pallas import tpu as pltpu
from jax.sharding import PartitionSpec as P

CAP = 16
MESH = pl.DeviceIdType.MESH
BF16 = jnp.bfloat16
F32 = jnp.float32


ORDERS = {
    4: [
        "B0a A1a B0b C0",
        "A1b B1a U0 V0",
        "A2a B1b C1 A2b",
        "B2a U1 A3a V1",
        "A3b B2b B3a C2",
        "A4ab B3b U2 V2",
        "B4a C3 B4b U3",
        "V3 C4 F3ba G3c",
        "U4 V4 F4ba G4c",
        "F2ba G2c G3b G3a",
        "H4c G4b G4a F1ba",
        "G1c H3c H4b H4a",
        "H3b H3a G2b G2a",
        "F0ba G0c H2c H2b",
        "H2a G1b H1c G1a",
        "H1b H1a H0c G0b",
        "G0a H0b H0a L0",
    ],
    1: [
        "B0ab A1ab B1ab C0",
        "U0 V0 C1 U1",
        "V1 F0ba G0c F1ba",
        "G1c G1ba H1cba G0ba",
        "H0cba L0",
    ],
    2: [
        "B0ab A1a C0 A1b",
        "B1a U0 V0 A2a",
        "B1b A2b C1 B2a",
        "B2b U1 V1 C2",
        "F1ba G1c U2 V2",
        "F2ba G2c F0ba G0c",
        "G1ba G2ba H2cba H1cba",
        "G0ba H0cba L0",
    ],
}


def kernel(
    nx,
    nz,
    d_early,
    r_early,
    order,
    tok_hbm,
    ids_ref,
    slot_ref,
    weight_ref,
    gate_hbm,
    up_hbm,
    down_hbm,
    out_ref,
    tokx,
    w1,
    wd,
    metas,
    pk,
    wt,
    zb,
    sel,
    xb,
    acc,
    hid,
    po,
    cr,
    ts,
    tr,
    ys,
    rb,
    zs,
    zr,
    last_out,
    last_in,
    w_sem,
    tok_sem,
    e_send,
    e_recv,
    last_send,
    last_recv,
    meta_send,
    meta_recv,
    zb_send,
    zb_recv,
    sel_send,
    sel_recv,
    sx_recv,
    t_send,
    t_recv,
    c_send,
    c_recv,
    ce_send,
    ce_recv,
    tt_send,
    tt_recv,
    r_send,
    r_recv,
    zr_send,
    zr_recv,
):
    expert = lax.axis_index("expert")
    tensor = lax.axis_index("tensor")
    z = lax.rem(expert, nz)
    yh = lax.rem(expert // nz, 2)
    x = expert // (2 * nz)
    c = lax.rem(tensor, 2)
    yl = tensor // 2
    half = nz // 2
    tok, width = tok_hbm.shape
    late_d = width - d_early
    d_whole = (pl.ds(0, late_d), pl.ds(late_d, 2 * d_early))
    own_late = pl.ds(0, late_d)
    own_head = pl.ds(late_d, d_early)
    extra = pl.ds(width, d_early)
    head = pl.ds(0, d_early)
    tail = pl.ds(d_early, late_d)
    late = width - r_early
    mid = late // 256 * 128
    r_count = 3
    r_whole = (pl.ds(0, mid), pl.ds(mid, late - mid), pl.ds(late, 2 * r_early))
    r_lates = (pl.ds(r_early, mid), pl.ds(r_early + mid, late - mid))
    r_head = pl.ds(0, r_early)

    def side(piece, count):
        return piece * 2 // count

    hidden = hid.shape[1]
    own_q = tensor
    far_q = (1 - yl) * 2 + c

    def at_z(d):
        return (expert - z + lax.rem(z + d + nz, nz), tensor)

    def at_plane(xx, rel):
        if rel == 0:
            return ((xx * 2 + yh) * nz + z, tensor)
        return ((xx * 2 + 1 - yh) * nz + z, (1 - yl) * 2 + c)

    t_peer = (expert, far_q)
    c_peer = (expert, yl * 2 + 1 - c)

    def blocks(s):
        if s == 0:
            return 0, 1
        if s == half:
            return nz - 1, 1
        return 2 * s - 1, 2

    def remote(src, dst, send, recv, dev):
        return pltpu.make_async_remote_copy(
            src_ref=src,
            dst_ref=dst,
            send_sem=send,
            recv_sem=recv,
            device_id=dev,
            device_id_type=MESH,
        )

    def wait_bytes(ref, sem):
        pltpu.make_async_copy(ref, ref, sem).wait()

    tok_loads = (
        pltpu.make_async_copy(tok_hbm.at[:, tail], tokx.at[:, own_late], tok_sem.at[0]),
        pltpu.make_async_copy(tok_hbm.at[:, head], tokx.at[:, own_head], tok_sem.at[1]),
    )
    for load in tok_loads:
        load.start()
    loads = []
    for q in range(4):
        rows = pl.ds(q * width, width)
        loads.append(
            pltpu.make_async_copy(
                gate_hbm.at[0, rows, :], w1.at[q, :, pl.ds(0, hidden)], w_sem.at[q]
            )
        )
        loads.append(
            pltpu.make_async_copy(
                up_hbm.at[0, rows, :], w1.at[q, :, pl.ds(hidden, hidden)], w_sem.at[4 + q]
            )
        )
        loads.append(
            pltpu.make_async_copy(down_hbm.at[0, :, rows], wd.at[q], w_sem.at[8 + q])
        )
    for load in loads:
        load.start()

    barrier = pltpu.get_barrier_semaphore()
    peers = [at_z(d) for d in range(1, nz)]
    peers += [at_plane(lax.rem(x + d, nx), 0) for d in range(1, nx)]
    peers += [at_plane(lax.rem(x + d, nx), 1) for d in range(nx)]
    peers += [t_peer, c_peer]
    for peer in peers:
        pl.semaphore_signal(barrier, inc=1, device_id=peer, device_id_type=MESH)

    metas[0, pl.ds(0, 8), :] = jnp.where(
        slot_ref[...] >= 0, ids_ref[...] * CAP + slot_ref[...], -1
    )
    metas[0, pl.ds(8, 8), :] = weight_ref[...]

    def delta(b):
        if b == 0:
            return 0
        if b == nz - 1:
            return half
        return (b + 1) // 2 if b % 2 == 1 else nz - b // 2

    seat = 2 * nx * CAP
    per_rel = nx * CAP

    def seat_codes():
        j = lax.broadcasted_iota(jnp.int32, (seat, tok), 0)
        rel = j // per_rel
        rest = j - rel * per_rel
        xe = rest // CAP
        slot = rest - xe * CAP
        far = yh + rel - 2 * yh * rel
        return ((xe * 2 + far) * nz + z) * CAP + slot

    def meta_copy(d):
        return remote(metas.at[0], metas.at[d], meta_send, meta_recv.at[d], at_z(d))

    def z_copy(s, way, piece):
        src = tokx if s == 1 else zb.at[2 * s - 3 + way]
        dst = zb.at[nz - 1] if s == half else zb.at[2 * s - 1 + way]
        cols = d_whole[piece]
        i = 2 * s + way
        return remote(
            src.at[:, cols], dst.at[:, cols], zb_send, zb_recv.at[i, piece], at_z(1 - 2 * way)
        )

    def z_parts(s, piece):
        return [z_copy(s, way, piece) for way in range(2) if s < half or way == side(piece, 2)]

    def z_send(s, piece):
        start_all(z_parts(s, piece))

    def start_all(copies):
        for copy in copies:
            copy.start()

    def routing(b):
        code = seat_codes()
        pick = jnp.zeros((seat, tok), F32)
        high = jnp.zeros((seat, tok), F32)
        low = jnp.zeros((seat, tok), F32)
        for k in range(8):
            hit = metas[delta(b), pl.ds(k, 1), :] == code
            weight = metas[delta(b), pl.ds(8 + k, 1), :]
            top = weight // 128
            pick = jnp.where(hit, 1.0, pick)
            high = jnp.where(hit, top.astype(F32) / 256.0, high)
            low = jnp.where(hit, (weight - top * 128).astype(F32) / 32768.0, low)
        pk[b] = pick.astype(BF16)
        wt[b, :, pl.ds(0, seat)] = high.T.astype(BF16)
        wt[b, :, pl.ds(seat, seat)] = low.T.astype(BF16)

    def pick_rows(b, cols):
        src = tokx[:, cols] if b == 0 else zb[b, :, cols]
        rows = jnp.dot(pk[b], src, preferred_element_type=F32).astype(BF16)
        sel[0, b, :, cols] = rows[:per_rel]
        sel[1, b, :, cols] = rows[per_rel:]

    mine = pl.ds(pl.multiple_of(x * CAP, CAP), CAP)

    def to_plane(s, cols, quarter, there, send, recv):
        bl = pl.ds(*blocks(s))
        pltpu.make_async_copy(
            sel.at[0, bl, mine, cols], xb.at[quarter, 0, bl, mine, there], recv(0)
        ).start()
        for rel in range(2):
            for d in range(1 - rel, nx):
                xx = lax.rem(x + d, nx)
                theirs = pl.ds(pl.multiple_of(xx * CAP, CAP), CAP)
                remote(
                    sel.at[rel, bl, theirs, cols],
                    xb.at[quarter, rel, bl, mine, there],
                    send(rel),
                    recv(rel),
                    at_plane(xx, rel),
                ).start()

    def send_piece(s, piece):
        send = lambda r: sel_send.at[r]
        if piece == 0:
            to_plane(s, own_late, own_q, tail, send, lambda r: sel_recv.at[s, r, 0])
        else:
            to_plane(s, own_head, own_q, head, send, lambda r: sel_recv.at[s, r, 1])
            to_plane(s, extra, far_q, head, send, lambda r: sx_recv.at[s, r])

    routing(0)
    for load in tok_loads:
        load.wait()
    pick_rows(0, d_whole[0])
    pl.semaphore_wait(barrier, len(peers))

    e_copy = remote(tokx.at[:, own_head], tokx.at[:, extra], e_send, e_recv, t_peer)
    start_all([e_copy])
    z_send(1, 0)
    send_piece(0, 0)
    for d in range(1, nz):
        meta_copy(d).start()
    for piece in range(1, 2):
        if piece == 2 - 1:
            e_copy.wait_recv()
        z_send(1, piece)
        pick_rows(0, d_whole[piece])
        send_piece(0, piece)

    def stage_a(s, piece):
        first, count = blocks(s)
        for copy in z_parts(s, piece):
            copy.wait_recv()
        if s < half:
            z_send(s + 1, piece)
        for b in range(first, first + count):
            if piece == 0:
                meta_copy(delta(b)).wait_recv()
                routing(b)
            pick_rows(b, d_whole[piece])
        send_piece(s, piece)

    def t_copies(s):
        bl = pl.ds(*blocks(s))
        out = []
        for rel in range(2):
            ref = xb.at[own_q if rel == 0 else far_q, rel, bl, :, tail]
            out.append(remote(ref, ref, t_send, t_recv.at[s, rel], t_peer))
        return out

    def c_copies(s, part):
        bl = pl.ds(*blocks(s))
        cols = (tail, head, head, tail)[part]
        out = []
        for rel in range(2):
            ref = xb.at[own_q if (rel == 0) == (part < 2) else far_q, rel, bl, :, cols]
            out.append(remote(ref, ref, c_send.at[part], c_recv.at[s, rel, part], c_peer))
        return out

    def stage_b(s, piece):
        bl = pl.ds(*blocks(s))
        for rel in range(2):
            near, far = (own_q, far_q) if rel == 0 else (far_q, own_q)
            cols = (tail, head)[piece]
            wait_bytes(xb.at[near, rel, bl, :, cols], sel_recv.at[s, rel, piece])
            if piece == 0:
                start_all([t_copies(s)[rel], c_copies(s, 0)[rel]])
            else:
                start_all([c_copies(s, 1)[rel]])
                wait_bytes(xb.at[far, rel, bl, :, head], sx_recv.at[s, rel])
                start_all([c_copies(s, 2)[rel]])

    def stage_c(s):
        t_list, c_list = t_copies(s), c_copies(s, 3)
        for rel in range(2):
            t_list[rel].wait_recv()
            start_all([c_list[rel]])

    def ce_copies(s):
        bl = pl.ds(*blocks(s))
        return [
            remote(
                po.at[2 * p + 1 - c, :, bl],
                cr.at[p, :, bl],
                ce_send,
                ce_recv.at[s, p],
                c_peer,
            )
            for p in range(2)
        ]

    loaded = {"w1": False, "wd": False}

    def stage_u(s):
        first, count = blocks(s)
        bl = pl.ds(first, count)
        rows = count * seat
        for part in range(4):
            for copy in c_copies(s, part):
                copy.wait_recv()
        if not loaded["w1"]:
            loaded["w1"] = True
            for load in loads:
                load.wait()

        xs = jnp.concatenate([xb[q, :, bl].reshape(rows, width) for q in range(4)], axis=1)
        ws = jnp.concatenate([w1[q] for q in range(4)], axis=0)
        acc[pl.ds(0, rows), :] = jnp.dot(xs, ws, preferred_element_type=F32)
        gate = acc[pl.ds(0, rows), pl.ds(0, hidden)]
        up = acc[pl.ds(0, rows), pl.ds(hidden, hidden)]
        hid[pl.ds(0, rows), :] = (gate / (1.0 + jnp.exp(-gate)) * up).astype(BF16)

    def stage_v(s):
        first, count = blocks(s)
        bl = pl.ds(first, count)
        rows = count * seat

        copies = ce_copies(s)
        for core in (1 - c, c):
            for p in range(2):
                q = 2 * p + core
                part = jnp.dot(hid[pl.ds(0, rows), :], wd[q], preferred_element_type=F32)
                po[q, :, bl] = part.astype(BF16).reshape(2, count, per_rel, width)
                start_all(copies[p : p + 1])
            copies = []

    def tt_copies(s, piece):
        bl = pl.ds(*blocks(s))
        cols = r_whole[piece]
        return [
            remote(
                ts.at[rel, bl, :, cols],
                tr.at[rel, bl, :, cols],
                tt_send,
                tt_recv.at[s, rel, piece],
                t_peer,
            )
            for rel in range(2)
        ]

    def cores(p, rel, bl, cols):
        ours = po[2 * p + c, rel, bl, :, cols].astype(F32)
        return ours + cr[p, rel, bl, :, cols].astype(F32)

    def stage_f(s, piece):
        bl = pl.ds(*blocks(s))
        copies = tt_copies(s, piece)
        if piece == 1:
            for copy in ce_copies(s):
                copy.wait_recv()
        for rel in range(2):
            p = 1 - yl if rel == 0 else yl
            ts[rel, bl, :, r_whole[piece]] = cores(p, rel, bl, r_lates[piece]).astype(BF16)
            start_all([copies[rel]])

    def stage_g(s, piece):
        bl = pl.ds(*blocks(s))
        copies = tt_copies(s, piece) if piece < 2 else None
        cols = r_whole[piece]
        for rel in range(2):
            p = yl if rel == 0 else 1 - yl
            if piece == 2:
                ys[rel, bl, :, pl.ds(late, r_early)] = cores(p, rel, bl, r_head).astype(BF16)
                ys[rel, bl, :, pl.ds(width, r_early)] = cores(1 - p, rel, bl, r_head).astype(BF16)
            else:
                copies[rel].wait_recv()
                total = cores(p, rel, bl, r_lates[piece]) + tr[rel, bl, :, cols].astype(F32)
                ys[rel, bl, :, cols] = total.astype(BF16)
            if rel == 0:
                pltpu.make_async_copy(
                    ys.at[0, bl, mine, cols], rb.at[0, bl, mine, cols], r_recv.at[s, 0, piece]
                ).start()
            for d in range(1 - rel, nx):
                xx = lax.rem(x + d, nx)
                theirs = pl.ds(pl.multiple_of(xx * CAP, CAP), CAP)
                remote(
                    ys.at[rel, bl, theirs, cols],
                    rb.at[rel, bl, mine, cols],
                    r_send.at[rel],
                    r_recv.at[s, rel, piece],
                    at_plane(xx, rel),
                ).start()
    def back_copy(s, way, piece):
        b = nz - 1 if s == half else 2 * s - 1 + way
        cols = r_whole[piece]
        i = 2 * s + way
        return remote(
            zs.at[b, :, cols], zr.at[b, :, cols], zr_send, zr_recv.at[i, piece], at_z(2 * way - 1)
        )

    last = remote(last_out, last_in, last_send, last_recv, t_peer)

    def stage_h(s, piece):
        first, count = blocks(s)
        cols = r_whole[piece]
        for rel in range(2):
            wait_bytes(rb.at[rel, pl.ds(first, count), :, cols], r_recv.at[s, rel, piece])
        for b in range(first, first + count):
            near, far = rb[0, b, :, cols], rb[1, b, :, cols]
            rows = jnp.concatenate([near, far, near, far], axis=0)
            total = jnp.dot(wt[b], rows, preferred_element_type=F32)
            for way in range(2) if s == 0 else (b - first,):
                if s == half or (s + 1 == half and way != side(piece, r_count)):
                    continue
                back_copy(s + 1, way, piece).wait_recv()
                src = nz - 1 if s + 1 == half else 2 * s + 1 + way
                total += zr[src, :, cols].astype(F32)
            if s > 0:
                zs[b, :, cols] = total.astype(BF16)
                start_all([back_copy(s, side(piece, r_count) if s == half else b - first, piece)])
            elif piece == 2:
                last_out[...] = total[:, r_early:].astype(BF16)
                start_all([last])
                acc[pl.ds(0, tok), r_head] = total[:, :r_early]
            else:
                out_ref[:, r_lates[piece]] = total.astype(BF16)

    def stage_l(s):
        last.wait_recv()
        both = acc[pl.ds(0, tok), r_head] + last_in[...].astype(F32)
        out_ref[:, r_head] = both.astype(BF16)

    stages = {
        "A": stage_a,
        "B": stage_b,
        "C": stage_c,
        "U": stage_u,
        "V": stage_v,
        "F": stage_f,
        "G": stage_g,
        "H": stage_h,
        "L": stage_l,
    }
    for name, *step in order:
        stages[name](*step)
    some = pl.ds(0, per_rel - CAP)
    e_copy.wait_send()
    last.wait_send()
    wait_bytes(metas.at[pl.ds(1, nz - 1)], meta_send)
    wait_bytes(zb.at[pl.ds(0, nz - 1)], zb_send)
    wait_bytes(zs.at[pl.ds(0, nz - 1)], zr_send)
    for ref, sem in ((sel, sel_send), (ys, r_send)):
        wait_bytes(ref.at[0, :, some, :], sem.at[0])
        wait_bytes(ref.at[1], sem.at[1])
    wait_bytes(xb.at[0, :, :, :, tail], t_send)
    wait_bytes(ts, tt_send)
    for part, cols in enumerate((tail, head, head, tail)):
        wait_bytes(xb.at[0, :, :, :, cols], c_send.at[part])
    wait_bytes(cr, ce_send)


def make_order(half):
    order = []
    for word in " ".join(ORDERS[half]).split():
        step = (word[0], int(word[1]))
        for piece in word[2:]:
            order.append(step + ("abcdef".index(piece),))
        if len(word) == 2:
            order.append(step)
    return order


def moe(nx, nz, d_early, r_early, tokens, ids, slots, weights, gate_weight, up_weight, down_weight):
    tok, width = tokens.shape
    hidden = gate_weight.shape[2]
    half = nz // 2
    chunks = half + 1
    per_rel = nx * CAP
    rows = 4 * per_rel
    dma = pltpu.SemaphoreType.DMA
    d_full, r_full = width + d_early, width + r_early
    vmem = pl.BlockSpec(memory_space=pltpu.VMEM)
    hbm = pl.BlockSpec(memory_space=pl.ANY)
    scratch = [
        pltpu.VMEM((tok, d_full), BF16),
        pltpu.VMEM((4, width, 2 * hidden), BF16),
        pltpu.VMEM((4, hidden, width), BF16),
        pltpu.VMEM((nz, 16, tok), jnp.int32),
        pltpu.VMEM((nz, 2 * per_rel, tok), BF16),
        pltpu.VMEM((nz, tok, 4 * per_rel), BF16),
        pltpu.VMEM((nz, tok, d_full), BF16),
        pltpu.VMEM((2, nz, per_rel, d_full), BF16),
        pltpu.VMEM((4, 2, nz, per_rel, width), BF16),
        pltpu.VMEM((rows, 2 * hidden), F32),
        pltpu.VMEM((rows, hidden), BF16),
        pltpu.VMEM((4, 2, nz, per_rel, width), BF16),
        pltpu.VMEM((2, 2, nz, per_rel, width), BF16),
        pltpu.VMEM((2, nz, per_rel, width - r_early), BF16),
        pltpu.VMEM((2, nz, per_rel, width - r_early), BF16),
        pltpu.VMEM((2, nz, per_rel, r_full), BF16),
        pltpu.VMEM((2, nz, per_rel, r_full), BF16),
        pltpu.VMEM((nz, tok, r_full), BF16),
        pltpu.VMEM((nz, tok, r_full), BF16),
        pltpu.VMEM((tok, r_early), BF16),
        pltpu.VMEM((tok, r_early), BF16),
        dma((12,)),
        dma((2,)),
        dma,
        dma,
        dma,
        dma,
        dma,
        dma((nz,)),
        dma,
        dma((2 * chunks, 2)),
        dma((2,)),
        dma((chunks, 2, 2)),
        dma((chunks, 2)),
        dma,
        dma((chunks, 2)),
        dma((4,)),
        dma((chunks, 2, 4)),
        dma,
        dma((chunks, 2)),
        dma,
        dma((chunks, 2, 3)),
        dma((2,)),
        dma((chunks, 2, 3)),
        dma,
        dma((2 * chunks, 3)),
    ]
    return pl.pallas_call(
        functools.partial(kernel, nx, nz, d_early, r_early, make_order(half)),
        out_shape=pltpu.VMEM((tok, width), BF16),
        in_specs=[hbm, vmem, vmem, vmem, hbm, hbm, hbm],
        out_specs=vmem,
        scratch_shapes=scratch,
        compiler_params=pltpu.CompilerParams(
            collective_id=0,
            has_side_effects=True,
            vmem_limit_bytes=60 * 1024 * 1024,
        ),
    )(tokens, ids, slots, weights, gate_weight, up_weight, down_weight)


def shards(nx, nz, d_early, r_early, tokens, expert_ids, slot_index, gate_fixed, *expert_weights):
    routing = (expert_ids.T, slot_index.T, gate_fixed.T)
    return moe(nx, nz, d_early, r_early, tokens, *routing, *expert_weights)


def solution(mesh, nx=4, nz=8, d_early=256, r_early=256):
    in_specs = (
        P("expert", "tensor"),
        P("expert", None),
        P("expert", None),
        P("expert", None),
        P("expert", None, "tensor"),
        P("expert", None, "tensor"),
        P("expert", "tensor", None),
    )
    return jax.shard_map(
        functools.partial(shards, nx, nz, d_early, r_early),
        mesh=mesh,
        in_specs=in_specs,
        out_specs=P("expert", "tensor"),
        check_vma=False,
    )
```
